128 devices in a mesh: seq: 32 (over y, x, core), head: 4 (over z).
Axes of the slice: x: 4, y: 4, z: 4, core: 2. Of those that a mesh axis runs over, the one named last changes fastest.
Arguments:
- queries: bfloat16 [32768, 8192], P('seq', 'head'), may hold values from -6 to 6
- key_rows: bfloat16 [32768, 8192], P('seq', 'head'), may hold values from -0.5 to 0.5
- value_rows: bfloat16 [32768, 8192], P('seq', 'head'), may hold values from -6 to 6
- log_decay: float32 [64, 32768], P('head', 'seq'), may hold values from -1 to 0, as said below
- gate_logits: bfloat16 [32768, 8192], P(('seq', 'head')), may hold values from -6 to 6
- norm_gain: float32 [8192], replicated, may hold values from 0.5 to 1.5
Outputs:
- gated_out: bfloat16 [32768, 8192], P(('seq', 'head'))
The draws below stay inside these ranges and needn't reach their ends.
Inputs may be any that keep to these rules, and one draw needn't show every extreme that they name: `log_decay`: log decays are negative.
All inputs are finite; a program needn't handle non-finite values.
Results may differ from the reference program's by a relative error of at most 0.0059.
Values may be sent and summed in bfloat16 or wider, within the bound.
A program may use at most 192 MiB of HBM per device.

```python
import jax
import jax.numpy as jnp
from jax import lax

HEAD_TOTAL = 64
HDIM = 128
BLOCK = 256
TOK_DEV = 1024
TOKEN_TOTAL = 32768
FEATURES = 8192


def draw_log_decay(key, part):
    random_key_parts = jax.random.split(key, 8)
    kind_draw = jax.random.uniform(random_key_parts[0], (HEAD_TOTAL,))
    slow_rate = jnp.exp(jax.random.uniform(random_key_parts[1], (HEAD_TOTAL,), minval=jnp.log(0.1), maxval=jnp.log(0.4))) / TOKEN_TOTAL
    fast_rate = jnp.exp(jax.random.uniform(random_key_parts[2], (HEAD_TOTAL,), minval=jnp.log(1.0 / 50.0), maxval=jnp.log(1.0 / 30.0)))
    middle_rate = jnp.exp(jax.random.uniform(random_key_parts[3], (HEAD_TOTAL,), minval=jnp.log(4.0 / TOKEN_TOTAL), maxval=jnp.log(1.0 / 30.0)))
    decay_rate = jnp.where(kind_draw < 0.5, slow_rate, jnp.where(kind_draw < 0.75, fast_rate, middle_rate))
    segments = TOKEN_TOTAL // TOK_DEV
    segment_factor = jnp.exp(jax.random.uniform(random_key_parts[4], (HEAD_TOTAL, segments), minval=jnp.log(0.5), maxval=jnp.log(2.0)))
    segment_factor = jnp.repeat(segment_factor, TOK_DEV, axis=1)
    position_factor = jax.random.uniform(random_key_parts[5], (HEAD_TOTAL, TOKEN_TOTAL), minval=0.5, maxval=1.5)
    spike_locations = jax.random.randint(random_key_parts[6], (2,), 0, TOKEN_TOTAL)
    spike_penalty = jax.random.uniform(random_key_parts[7], (HEAD_TOTAL, 2), minval=0.2, maxval=0.4)
    token_places = jnp.arange(TOKEN_TOTAL)
    initial_spike = jnp.where(token_places[None, :] == spike_locations[0], jnp.log(1.0 - spike_penalty[:, 0:1]), 0.0)
    followup_spike = jnp.where(token_places[None, :] == spike_locations[1], jnp.log(1.0 - spike_penalty[:, 1:2]), 0.0)
    stable_baseline = -decay_rate[:, None] * segment_factor * position_factor
    return (stable_baseline + initial_spike + followup_spike).astype(jnp.float32)


def block_scale(own_key, extent, pieces, low, top_value):
    def one(axis_at, shards_of):
        draws = jax.random.uniform(jax.random.fold_in(jax.random.fold_in(own_key, 6), axis_at), (shards_of,), jnp.float32, low / len(pieces), top_value / len(pieces))
        return jnp.repeat(jnp.exp(draws), extent[axis_at] // shards_of).reshape((-1,) + (1,) * (len(extent) - axis_at - 1))

    gain = one(*pieces[0])
    for cut in pieces[1:]:
        gain = gain * one(*cut)
    return gain


def gaussian(rng, shape, scale, reach, cuts=(), kind=jnp.bfloat16):
    level = block_scale(rng, shape, cuts, -0.22, 0.18) if cuts else 1.0
    values = jax.random.normal(rng, shape, jnp.float32) * scale * level
    return jnp.minimum(jnp.maximum(values, -reach), reach).astype(kind)


def setup_inputs(seed: int = 0) -> dict:
    streams_of = jax.random.split(jax.random.key(seed), 7)
    queries = gaussian(streams_of[0], (TOKEN_TOTAL, FEATURES), 1.0, 6.0, ((0, 32), (1, 4)))
    key_rows = gaussian(streams_of[1], (TOKEN_TOTAL, FEATURES), (HDIM ** -0.5), 0.5, ((0, 32), (1, 4)))
    value_rows = gaussian(streams_of[2], (TOKEN_TOTAL, FEATURES), 1.0, 6.0, ((0, 32), (1, 4)))
    log_decay = draw_log_decay(jax.random.fold_in(streams_of[6], 71), 0)
    gate_logits = gaussian(streams_of[4], (TOKEN_TOTAL, FEATURES), 1.0, 6.0, ((0, 128),))
    norm_gain = jnp.clip(1.0 + 0.1 * jax.random.normal(streams_of[5], (FEATURES,), jnp.float32), 0.5, 1.5)
    return {"queries": queries, "key_rows": key_rows, "value_rows": value_rows, "log_decay": log_decay, "gate_logits": gate_logits, "norm_gain": norm_gain}


norm_eps = 1e-06

def block_step(prefix_state, inputs):
    query_block, key_block, value_block, cumulative = inputs
    highest = lax.Precision.HIGHEST
    state_bf16 = lax.optimization_barrier(prefix_state.astype(jnp.bfloat16))
    query_wide = query_block.astype(jnp.float32)
    value_wide = value_block.astype(jnp.float32)
    carried = jnp.einsum('thd,hde->the', query_wide, state_bf16.astype(jnp.float32), precision=highest)
    carried = carried * jnp.exp(cumulative).T[:, :, None]
    scores = jnp.einsum('thd,shd->hts', query_wide, key_block.astype(jnp.float32), precision=highest)
    length = cumulative.shape[1]
    lower_mask = jnp.tril(jnp.ones((length, length), dtype=bool))[None]
    spread = cumulative[:, :, None] - cumulative[:, None, :]
    weights = jnp.where(lower_mask, scores * jnp.exp(jnp.where(lower_mask, spread, 0.0)), 0.0)
    weights = lax.optimization_barrier(weights.astype(jnp.bfloat16))
    within = jnp.einsum('hts,she->the', weights.astype(jnp.float32), value_wide, precision=highest)
    attended = (within + carried).astype(jnp.bfloat16)
    block_end = cumulative[:, -1]
    weighted_keys = key_block.astype(jnp.float32) * jnp.exp(block_end[:, None] - cumulative).T[:, :, None]
    weighted_keys = lax.optimization_barrier(weighted_keys.astype(jnp.bfloat16))
    block_state = jnp.einsum('thd,the->hde', weighted_keys.astype(jnp.float32), value_wide, precision=highest)
    next_state = jnp.exp(block_end)[:, None, None] * prefix_state + block_state
    return (next_state, attended)

def reference(queries, key_rows, value_rows, log_decay, gate_logits, norm_gain):
    block_total = TOKEN_TOTAL // BLOCK
    query_blocks = queries.reshape(block_total, BLOCK, HEAD_TOTAL, HDIM)
    key_blocks = key_rows.reshape(block_total, BLOCK, HEAD_TOTAL, HDIM)
    value_blocks = value_rows.reshape(block_total, BLOCK, HEAD_TOTAL, HDIM)
    cumulative = jnp.cumsum(log_decay.reshape(HEAD_TOTAL, block_total, BLOCK), axis=2).transpose(1, 0, 2)
    start_state = jnp.zeros((HEAD_TOTAL, HDIM, HDIM), jnp.float32)
    final_state, attended = lax.scan(block_step, start_state, (query_blocks, key_blocks, value_blocks, cumulative))
    widened = attended.reshape(TOKEN_TOTAL, HEAD_TOTAL * HDIM).astype(jnp.float32)
    mean_square = lax.optimization_barrier(jnp.mean(widened * widened, axis=1, keepdims=True))
    normed = widened * lax.rsqrt(mean_square + norm_eps) * norm_gain[None, :]
    return (normed * jax.nn.sigmoid(gate_logits.astype(jnp.float32))).astype(jnp.bfloat16)
```

```python
import jax
import jax.numpy as jnp
from jax import lax
from jax.experimental import pallas as pl
from jax.experimental.pallas import tpu as pltpu
from jax.sharding import PartitionSpec as P

BLOCK = 256
HALF = 128
WIDTH = 128
norm_eps = 1e-06

MESH = pl.DeviceIdType.MESH
F32 = jnp.float32
BF16 = jnp.bfloat16
EXACT = lax.Precision.HIGHEST

NX = 4
NY = 4
AHEAD = 3
LAG_Y = 4
LAG_RET = 7
LAG_ATT = 8
TAIL_PARTS = ((128, 64), (192, 32), (224, 32))


def make_kernel(heads, blocks, z_count):
    groups = heads // 2
    features = heads * WIDTH

    def kernel(
        q_hbm, k_hbm, v_hbm, ld_ref, gate_hbm, gain_ref, out_ref,
        qv, kv, vv, gv, gs, att, recv, cum_row, cum_col, col, loc, start, tot, pair_in, xb, yb, prow, sret, sin,
        dec, dsib, dx, dy,
        load_sem, gate_sem, out_sem, own_sem,
        pair_s, pair_r, x_s, x_r, y_s, y_r, ret_s, ret_r, z_s, z_r,
        dp_s, dp_r, dx_s, dx_r, dy_s, dy_r,
    ):
        seq = lax.axis_index("seq")
        z = lax.axis_index("head")
        core = lax.rem(seq, 2)
        x = lax.rem(seq // 2, NX)
        y = seq // (2 * NX)
        sibling = seq + 1 - 2 * core

        def x_peer(d):
            return (y * NX + lax.rem(x + d, NX)) * 2 + core

        def y_peer(d):
            return (lax.rem(y + d, NY) * NX + x) * 2 + core

        def z_peer(d):
            return lax.rem(z + d, z_count)

        def send(src, dst, s, r, axis, dev):
            return pltpu.make_async_remote_copy(
                src_ref=src, dst_ref=dst, send_sem=s, recv_sem=r, device_id={axis: dev}, device_id_type=MESH
            )

        def load(i, src, dst, h):
            return pltpu.make_async_copy(src.at[:, pl.ds(pl.multiple_of(h * WIDTH, WIDTH), WIDTH)], dst.at[h], load_sem.at[i, h])

        barrier = pltpu.get_barrier_semaphore()
        pl.semaphore_signal(barrier, inc=1, device_id={"seq": sibling}, device_id_type=MESH)
        for d in range(1, NX):
            pl.semaphore_signal(barrier, inc=1, device_id={"seq": x_peer(d)}, device_id_type=MESH)
        for d in range(1, NY):
            pl.semaphore_signal(barrier, inc=1, device_id={"seq": y_peer(d)}, device_id_type=MESH)
        for d in range(1, z_count):
            pl.semaphore_signal(barrier, inc=1, device_id={"head": z_peer(d)}, device_id_type=MESH)

        @pl.loop(0, heads)
        def _(h):
            load(0, k_hbm, kv, h).start()
            load(1, v_hbm, vv, h).start()

        @pl.loop(0, heads)
        def _(h):
            load(2, q_hbm, qv, h).start()

        gate_copy = pltpu.make_async_copy(gate_hbm, gv, gate_sem)
        gate_copy.start()

        t_at = lax.broadcasted_iota(jnp.int32, (BLOCK, BLOCK), 0)
        s_at = lax.broadcasted_iota(jnp.int32, (BLOCK, BLOCK), 1)
        lower = (s_at <= t_at).astype(F32)
        upper = (t_at <= s_at).astype(F32)
        for b in range(blocks):
            ld = ld_ref[:, b * BLOCK : (b + 1) * BLOCK]
            running = jnp.dot(ld, upper, precision=EXACT, preferred_element_type=F32)
            cum_row[b, 0] = running[:, :HALF]
            cum_row[b, 1] = running[:, HALF:]
            padded = jnp.concatenate([ld, jnp.zeros((WIDTH - heads, BLOCK), F32)], axis=0)
            cum_col[b] = lax.dot_general(
                lower, padded, (((1,), (1,)), ((), ())), precision=EXACT, preferred_element_type=F32
            )
        dec[...] = jnp.dot(
            ld_ref[...], jnp.ones((blocks * BLOCK, WIDTH), F32), precision=EXACT, preferred_element_type=F32
        )

        def states(g):
            for i in range(2):
                h = 2 * g + i
                load(0, k_hbm, kv, h).wait()
                load(1, v_hbm, vv, h).wait()

                def block(b, run):
                    turned = pltpu.roll(cum_col[b], lax.rem(WIDTH - h, WIDTH), 1)
                    c = jnp.broadcast_to(turned[:, :1], (BLOCK, WIDTH))
                    col[h, b] = c
                    end = c[BLOCK - 1 :, :]
                    rows = pl.ds(pl.multiple_of(b * BLOCK, BLOCK), BLOCK)
                    weighted = (kv[h, rows, :].astype(F32) * jnp.exp(end - c)).astype(BF16)
                    piece = lax.dot_general(
                        weighted, vv[h, rows, :], (((0,), (0,)), ((), ())), preferred_element_type=F32
                    )
                    loc[h, b] = run
                    return jnp.exp(end) * run + piece

                tot[h] = lax.fori_loop(0, blocks, block, jnp.zeros((WIDTH, WIDTH), F32))

        def pair_copy(g):
            return send(tot.at[2 * g + 1 - core], pair_in.at[g], pair_s.at[g], pair_r.at[g], "seq", sibling)

        def x_copy(g, d):
            return send(xb.at[g, x], xb.at[g, x], x_s.at[g, d - 1], x_r.at[g, d - 1], "seq", x_peer(d))

        def x_got(g, d):
            at = lax.rem(x + NX - d, NX)
            return send(xb.at[g, at], xb.at[g, at], x_s.at[g, d - 1], x_r.at[g, d - 1], "seq", x_peer(d))

        def y_copy(g, d):
            return send(yb.at[g, y], yb.at[g, y], y_s.at[g, d - 1], y_r.at[g, d - 1], "seq", y_peer(d))

        def y_got(g, d):
            at = lax.rem(y + NY - d, NY)
            return send(yb.at[g, at], yb.at[g, at], y_s.at[g, d - 1], y_r.at[g, d - 1], "seq", y_peer(d))

        def ret_copy(g):
            return send(sret.at[g], sin.at[2 * g + core], ret_s.at[g], ret_r.at[g], "seq", sibling)

        def ret_got(g):
            return send(sret.at[g], sin.at[2 * g + 1 - core], ret_s.at[g], ret_r.at[g], "seq", sibling)

        dec_pair = send(dec, dsib, dp_s, dp_r, "seq", sibling)

        def dx_copy(d):
            return send(dx.at[x], dx.at[x], dx_s.at[d - 1], dx_r.at[d - 1], "seq", x_peer(d))

        def dx_got(d):
            at = lax.rem(x + NX - d, NX)
            return send(dx.at[at], dx.at[at], dx_s.at[d - 1], dx_r.at[d - 1], "seq", x_peer(d))

        def dy_copy(d):
            return send(dy.at[y], dy.at[y], dy_s.at[d - 1], dy_r.at[d - 1], "seq", y_peer(d))

        def dy_got(d):
            at = lax.rem(y + NY - d, NY)
            return send(dy.at[at], dy.at[at], dy_s.at[d - 1], dy_r.at[d - 1], "seq", y_peer(d))

        def between(rows, lo, hi):
            total = jnp.zeros((1, WIDTH), F32)
            for i in range(lo + 1, len(rows)):
                total = total + jnp.where(i < hi, rows[i], 0.0)
            return total

        def own_core(g):
            h = 2 * g + core
            mine, other = tot[h], pair_in[g]
            here, there = dec[pl.ds(h, 1), :], dsib[pl.ds(h, 1), :]
            first = core == 0
            return (
                h,
                jnp.where(first, mine, other),
                jnp.where(first, other, mine),
                jnp.where(first, here, there),
                jnp.where(first, there, here),
            )

        def pair_step(g):
            pair_copy(g).wait_recv()

            @pl.when(g == 0)
            def _():
                dec_pair.wait_recv()
                dx[x] = dec[...] + dsib[...]
                for d in range(1, NX):
                    dx_copy(d).start()

            h, first, second, _, second_decay = own_core(g)
            xb[g, x] = (jnp.exp(second_decay) * first + second).astype(xb.dtype)
            for d in range(1, NX):
                x_copy(g, d).start()

        def x_rows(h):
            return [dx[i, pl.ds(h, 1), :] for i in range(NX)]

        def row_step(g):
            @pl.when(g == 0)
            def _():
                for d in range(1, NX):
                    dx_got(d).wait_recv()
                dy[y] = dx[0] + dx[1] + dx[2] + dx[3]
                for d in range(1, NY):
                    dy_copy(d).start()

            for d in range(1, NX):
                x_got(g, d).wait_recv()
            h = 2 * g + core
            rows = x_rows(h)
            whole = jnp.zeros((WIDTH, WIDTH), F32)
            before = jnp.zeros((WIDTH, WIDTH), F32)
            for i in range(NX):
                piece = xb[g, i].astype(F32)
                whole = whole + jnp.exp(between(rows, i, NX)) * piece
                before = before + jnp.where(i < x, jnp.exp(between(rows, i, x)), 0.0) * piece
            prow[g] = before
            yb[g, y] = whole.astype(yb.dtype)
            for d in range(1, NY):
                y_copy(g, d).start()

        def return_step(g):
            @pl.when(g == 0)
            def _():
                for d in range(1, NY):
                    dy_got(d).wait_recv()

            for d in range(1, NY):
                y_got(g, d).wait_recv()
            h, first, _, first_decay, _ = own_core(g)
            rows = [dy[i, pl.ds(h, 1), :] for i in range(NY)]
            above = jnp.zeros((WIDTH, WIDTH), F32)
            for i in range(NY):
                above = above + jnp.where(i < y, jnp.exp(between(rows, i, y)), 0.0) * yb[g, i].astype(F32)
            at_first = jnp.exp(between(x_rows(h), -1, x)) * above + prow[g]
            at_second = jnp.exp(first_decay) * at_first + first
            sin[h] = jnp.where(core == 0, at_first, at_second)
            sret[g] = jnp.where(core == 0, at_second, at_first)
            ret_copy(g).start()

        def z_copy(g, part, r0, rows, d):
            p = z_peer(d)
            src = pl.ds(pl.multiple_of(g * 2 * WIDTH, 2 * WIDTH), 2 * WIDTH)
            dst = pl.ds(pl.multiple_of(z * features + g * 2 * WIDTH, 2 * WIDTH), 2 * WIDTH)
            return send(
                att.at[p, pl.ds(r0, rows), src], recv.at[pl.ds(r0, rows), dst],
                z_s.at[part, g, d - 1], z_r.at[part, g, d - 1], "head", p,
            )

        def z_got(g, part, r0, rows, d):
            src = pl.ds(pl.multiple_of(g * 2 * WIDTH, 2 * WIDTH), 2 * WIDTH)
            origin = lax.rem(z + z_count - d, z_count)
            dst = pl.ds(pl.multiple_of(origin * features + g * 2 * WIDTH, 2 * WIDTH), 2 * WIDTH)
            return send(
                att.at[z_peer(d), pl.ds(r0, rows), src], recv.at[pl.ds(r0, rows), dst],
                z_s.at[part, g, d - 1], z_r.at[part, g, d - 1], "head", z_peer(d),
            )

        def own_copy(g, part, r0, rows):
            src = pl.ds(pl.multiple_of(g * 2 * WIDTH, 2 * WIDTH), 2 * WIDTH)
            dst = pl.ds(pl.multiple_of(z * features + g * 2 * WIDTH, 2 * WIDTH), 2 * WIDTH)
            return pltpu.make_async_copy(
                att.at[z, pl.ds(r0, rows), src], recv.at[pl.ds(r0, rows), dst], own_sem.at[part, g]
            )

        def ship(g, part, r0, rows):
            for d in (2, 1, 3):
                z_copy(g, part, r0, rows, d).start()
            own_copy(g, part, r0, rows).start()

        def arrived(part, r0, rows):
            @pl.loop(0, groups)
            def _(g):
                for d in range(1, z_count):
                    z_got(g, part, r0, rows, d).wait_recv()
                own_copy(g, part, r0, rows).wait()

        def attend_first(g):
            ret_got(g).wait_recv()
            for i in range(2):
                h = 2 * g + i
                load(2, q_hbm, qv, h).wait()

                def block(b, gone):
                    c = col[h, b, :HALF, :]
                    begin = (jnp.exp(gone) * sin[h] + loc[h, b]).astype(BF16)
                    start[h, b] = begin
                    rows = pl.ds(pl.multiple_of(b * BLOCK, BLOCK), HALF)
                    q = qv[h, rows, :]
                    scores = lax.dot_general(q, kv[h, rows, :], (((1,), (1,)), ((), ())), preferred_element_type=F32)
                    keep = lax.broadcasted_iota(jnp.int32, (HALF, HALF), 1) <= lax.broadcasted_iota(
                        jnp.int32, (HALF, HALF), 0
                    )
                    spread = jnp.where(keep, c - cum_row[b, 0, pl.ds(h, 1), :], 0.0)
                    weights = jnp.where(keep, scores * jnp.exp(spread), 0.0).astype(BF16)
                    within = jnp.dot(weights, vv[h, rows, :], preferred_element_type=F32)
                    carried = jnp.dot(q, begin, preferred_element_type=F32) * jnp.exp(c)
                    att[b, :HALF, pl.ds(pl.multiple_of(h * WIDTH, WIDTH), WIDTH)] = (within + carried).astype(BF16)
                    return gone + col[h, b, BLOCK - 1 :, :]

                lax.fori_loop(0, blocks, block, jnp.zeros((1, WIDTH), F32))
            ship(g, 0, 0, HALF)

        def attend_second(g):
            for i in range(2):
                h = 2 * g + i

                @pl.loop(0, blocks)
                def _(b):
                    c = col[h, b, HALF:, :]
                    top = pl.multiple_of(b * BLOCK, BLOCK)
                    rows = pl.ds(top, BLOCK)
                    q = qv[h, pl.ds(pl.multiple_of(top + HALF, HALF), HALF), :]
                    scores = lax.dot_general(q, kv[h, rows, :], (((1,), (1,)), ((), ())), preferred_element_type=F32)
                    keep = lax.broadcasted_iota(jnp.int32, (HALF, BLOCK), 1) <= HALF + lax.broadcasted_iota(
                        jnp.int32, (HALF, BLOCK), 0
                    )
                    wide = jnp.concatenate([c, c], axis=1)
                    key_cum = jnp.concatenate([cum_row[b, j, pl.ds(h, 1), :] for j in range(2)], axis=1)
                    spread = jnp.where(keep, wide - key_cum, 0.0)
                    weights = jnp.where(keep, scores * jnp.exp(spread), 0.0).astype(BF16)
                    within = jnp.dot(weights, vv[h, rows, :], preferred_element_type=F32)
                    carried = jnp.dot(q, start[h, b], preferred_element_type=F32) * jnp.exp(c)
                    att[b, HALF:, pl.ds(pl.multiple_of(h * WIDTH, WIDTH), WIDTH)] = (within + carried).astype(BF16)

            ship(g, 1, *TAIL_PARTS[0])

        span = 1024
        chunks = z_count * features // span

        def gates():
            @pl.loop(0, BLOCK // 16)
            def _(i):
                rows = pl.ds(pl.multiple_of(i * 16, 16), 16)
                for j in range(chunks):
                    lanes = slice(j * span, (j + 1) * span)
                    gs[rows, lanes] = gain_ref[:, lanes] * jax.nn.sigmoid(gv[rows, lanes].astype(F32))

        def norm(r0, count):
            @pl.loop(0, count // 16)
            def _(i):
                rows = pl.ds(pl.multiple_of(r0 + i * 16, 16), 16)
                total = jnp.zeros((16, span), F32)
                for j in range(chunks):
                    wide = recv[rows, j * span : (j + 1) * span].astype(F32)
                    total = total + wide * wide
                mean = jnp.sum(total, axis=1, keepdims=True) * (1.0 / (z_count * features))
                scale = lax.rsqrt(mean + norm_eps)
                for j in range(chunks):
                    lanes = slice(j * span, (j + 1) * span)
                    recv[rows, lanes] = (recv[rows, lanes].astype(F32) * scale * gs[rows, lanes]).astype(BF16)

        def out_copy(part, r0, rows):
            return pltpu.make_async_copy(recv.at[pl.ds(r0, rows)], out_ref.at[pl.ds(r0, rows)], out_sem.at[part])

        for g in range(AHEAD):
            states(g)
        pl.semaphore_wait(barrier, 1 + (NX - 1) + (NY - 1) + (z_count - 1))
        dec_pair.start()

        @pl.loop(0, LAG_ATT + groups)
        def _(k):
            @pl.when(k < groups)
            def _():
                pair_copy(k).start()

            @pl.when(k >= LAG_ATT)
            def _():
                attend_first(k - LAG_ATT)

            @pl.when((k >= LAG_RET) & (k < LAG_RET + groups))
            def _():
                return_step(k - LAG_RET)

            @pl.when((k >= LAG_Y) & (k < LAG_Y + groups))
            def _():
                row_step(k - LAG_Y)

            @pl.when((k >= 1) & (k < 1 + groups))
            def _():
                pair_step(k - 1)

            @pl.when(k + AHEAD < groups)
            def _():
                states(k + AHEAD)

        @pl.loop(0, groups)
        def _(g):
            attend_second(g)

        for part in range(1, len(TAIL_PARTS)):
            r0, rows = TAIL_PARTS[part]

            @pl.loop(0, groups)
            def _(g):
                ship(g, part + 1, r0, rows)

        gate_copy.wait()
        gates()
        parts = ((0, HALF),) + TAIL_PARTS
        for part, (r0, rows) in enumerate(parts):
            arrived(part, r0, rows)
            norm(r0, rows)
            out_copy(part, r0, rows).start()

        dec_pair.wait_send()
        for d in range(1, NX):
            dx_copy(d).wait_send()
        for d in range(1, NY):
            dy_copy(d).wait_send()

        @pl.loop(0, groups)
        def _(g):
            pair_copy(g).wait_send()
            for d in range(1, NX):
                x_copy(g, d).wait_send()
            for d in range(1, NY):
                y_copy(g, d).wait_send()
            ret_copy(g).wait_send()
            for part, (r0, rows) in enumerate(parts):
                for d in range(1, z_count):
                    z_copy(g, part, r0, rows, d).wait_send()

        for part, (r0, rows) in enumerate(parts):
            out_copy(part, r0, rows).wait()

    return kernel


def solution(mesh):
    z_count = mesh.shape["head"]

    def on_device(queries, key_rows, value_rows, log_decay, gate_logits, norm_gain):
        local, features = queries.shape
        heads = log_decay.shape[0]
        blocks = local // BLOCK
        groups = heads // 2
        rows, wide = gate_logits.shape
        parts = 1 + len(TAIL_PARTS)
        vmem, dma = pltpu.VMEM, pltpu.SemaphoreType.DMA
        state = (WIDTH, WIDTH)
        return pl.pallas_call(
            make_kernel(heads, blocks, z_count),
            out_shape=jax.ShapeDtypeStruct((rows, wide), BF16),
            in_specs=[
                pl.BlockSpec(memory_space=pl.ANY),
                pl.BlockSpec(memory_space=pl.ANY),
                pl.BlockSpec(memory_space=pl.ANY),
                pl.BlockSpec(memory_space=pltpu.VMEM),
                pl.BlockSpec(memory_space=pl.ANY),
                pl.BlockSpec(memory_space=pltpu.VMEM),
            ],
            out_specs=pl.BlockSpec(memory_space=pl.ANY),
            scratch_shapes=[
                vmem((heads, local, WIDTH), BF16),
                vmem((heads, local, WIDTH), BF16),
                vmem((heads, local, WIDTH), BF16),
                vmem((rows, wide), BF16),
                vmem((rows, wide), F32),
                vmem((z_count, rows, features), BF16),
                vmem((rows, wide), BF16),
                vmem((blocks, 2, heads, HALF), F32),
                vmem((blocks, BLOCK, WIDTH), F32),
                vmem((heads, blocks, BLOCK, WIDTH), F32),
                vmem((heads, blocks) + state, F32),
                vmem((heads, blocks) + state, BF16),
                vmem((heads,) + state, F32),
                vmem((groups,) + state, F32),
                vmem((groups, NX) + state, BF16),
                vmem((groups, NY) + state, BF16),
                vmem((groups,) + state, F32),
                vmem((groups,) + state, F32),
                vmem((heads,) + state, F32),
                vmem((heads, WIDTH), F32),
                vmem((heads, WIDTH), F32),
                vmem((NX, heads, WIDTH), F32),
                vmem((NY, heads, WIDTH), F32),
                dma((3, heads)),
                dma,
                dma((parts,)),
                dma((parts, groups)),
                dma((groups,)),
                dma((groups,)),
                dma((groups, NX - 1)),
                dma((groups, NX - 1)),
                dma((groups, NY - 1)),
                dma((groups, NY - 1)),
                dma((groups,)),
                dma((groups,)),
                dma((parts, groups, z_count - 1)),
                dma((parts, groups, z_count - 1)),
                dma,
                dma,
                dma((NX - 1,)),
                dma((NX - 1,)),
                dma((NY - 1,)),
                dma((NY - 1,)),
            ],
            compiler_params=pltpu.CompilerParams(
                collective_id=0, has_side_effects=True, vmem_limit_bytes=56 * 2**20
            ),
        )(queries, key_rows, value_rows, log_decay, gate_logits, norm_gain[None, :])

    placed = (
        P("seq", "head"),
        P("seq", "head"),
        P("seq", "head"),
        P("head", "seq"),
        P(("seq", "head"), None),
        P(),
    )
    return jax.shard_map(
        on_device, mesh=mesh, in_specs=placed, out_specs=P(("seq", "head"), None), check_vma=False
    )
```

```python
import jax
import jax.numpy as jnp
from jax import lax
from jax.experimental import pallas as pl
from jax.experimental.pallas import tpu as pltpu
from jax.sharding import PartitionSpec as P

BLOCK = 256
HALF = 128
WIDTH = 128
norm_eps = 1e-06

MESH = pl.DeviceIdType.MESH
F32 = jnp.float32
BF16 = jnp.bfloat16

NX = 4
NY = 4
AHEAD = 3
LAG_Y = 4
LAG_RET = 7
LAG_ATT = 8
TAIL_PARTS = ((128, 64), (192, 32), (224, 32))


def make_kernel(heads, blocks, z_count):
    groups = heads // 2
    features = heads * WIDTH

    def kernel(
        q_hbm, k_hbm, v_hbm, ld_hbm, gate_hbm, gain_hbm, out_ref,
        qb, kvb, gv, ld_ref, gain_ref, att, recv, cum_row, cum_col, col, loc, start, tot, pair_in, xb, yb, prow, sret, sin,
        dec, dsib, dx, dy,
        kv_sem, q_sem, ld_sem, gain_sem, gate_sem, out_sem, own_sem,
        pair_s, pair_r, x_s, x_r, y_s, y_r, ret_s, ret_r, z_s, z_r,
        dp_s, dp_r, dx_s, dx_r, dy_s, dy_r,
    ):
        seq = lax.axis_index("seq")
        z = lax.axis_index("head")
        core = lax.rem(seq, 2)
        x = lax.rem(seq // 2, NX)
        y = seq // (2 * NX)
        sibling = seq + 1 - 2 * core

        def x_peer(d):
            return (y * NX + lax.rem(x + d, NX)) * 2 + core

        def y_peer(d):
            return (lax.rem(y + d, NY) * NX + x) * 2 + core

        def z_peer(d):
            return lax.rem(z + d, z_count)

        def send(src, dst, s, r, axis, dev):
            return pltpu.make_async_remote_copy(
                src_ref=src, dst_ref=dst, send_sem=s, recv_sem=r, device_id={axis: dev}, device_id_type=MESH
            )

        def got(ref, sem):
            pltpu.make_async_copy(ref, ref, sem).wait()

        def pair_lanes(g):
            return pl.ds(pl.multiple_of(g * 2 * WIDTH, 2 * WIDTH), 2 * WIDTH)

        barrier = pltpu.get_barrier_semaphore()
        pl.semaphore_signal(barrier, inc=1, device_id={"seq": sibling}, device_id_type=MESH)
        for d in range(1, NX):
            pl.semaphore_signal(barrier, inc=1, device_id={"seq": x_peer(d)}, device_id_type=MESH)
        for d in range(1, NY):
            pl.semaphore_signal(barrier, inc=1, device_id={"seq": y_peer(d)}, device_id_type=MESH)
        for d in range(1, z_count):
            pl.semaphore_signal(barrier, inc=1, device_id={"head": z_peer(d)}, device_id_type=MESH)

        ld_copy = pltpu.make_async_copy(ld_hbm, ld_ref, ld_sem)
        ld_copy.start()

        @pl.loop(0, groups)
        def _(g):
            pltpu.make_async_copy(k_hbm.at[:, pair_lanes(g)], kvb.at[g, 0], kv_sem.at[g]).start()
            pltpu.make_async_copy(v_hbm.at[:, pair_lanes(g)], kvb.at[g, 1], kv_sem.at[g]).start()

        @pl.loop(0, groups)
        def _(g):
            pltpu.make_async_copy(q_hbm.at[:, pair_lanes(g)], qb.at[g], q_sem.at[g]).start()

        gain_copy = pltpu.make_async_copy(gain_hbm, gain_ref, gain_sem)
        gain_copy.start()
        gate_copy = pltpu.make_async_copy(gate_hbm, gv, gate_sem)
        gate_copy.start()

        t_at = lax.broadcasted_iota(jnp.int32, (BLOCK, BLOCK), 0)
        s_at = lax.broadcasted_iota(jnp.int32, (BLOCK, BLOCK), 1)
        lower = (s_at <= t_at).astype(BF16)
        upper = (t_at <= s_at).astype(BF16)

        def thirds(wide):
            pieces = []
            for _ in range(3):
                pieces.append(wide.astype(BF16))
                wide = wide - pieces[-1].astype(F32)
            return pieces

        def add_up(pieces, one):
            return one(pieces[2]) + one(pieces[1]) + one(pieces[0])

        ld_copy.wait()
        ld = thirds(jnp.concatenate([ld_ref[:, b * BLOCK : (b + 1) * BLOCK] for b in range(blocks)], axis=0))
        running = add_up(ld, lambda p: jnp.dot(p, upper, preferred_element_type=F32))
        for b in range(blocks):
            cum_row[b, 0] = running[b * heads : (b + 1) * heads, :HALF]
            cum_row[b, 1] = running[b * heads : (b + 1) * heads, HALF:]
        blank = jnp.zeros((WIDTH - blocks * heads, BLOCK), BF16)
        cum_col[...] = add_up(
            ld,
            lambda p: lax.dot_general(
                lower, jnp.concatenate([p, blank], axis=0), (((1,), (1,)), ((), ())), preferred_element_type=F32
            ),
        )
        ends = add_up(ld, lambda p: jnp.dot(p, jnp.ones((BLOCK, WIDTH), BF16), preferred_element_type=F32))
        total = ends[:heads]
        for b in range(1, blocks):
            total = total + ends[b * heads : (b + 1) * heads]
        dec[...] = total

        def states(g):
            got(kvb.at[g], kv_sem.at[g])
            runs = [jnp.zeros((WIDTH, WIDTH), F32)] * 2
            for b in range(blocks):
                rows = slice(b * BLOCK, (b + 1) * BLOCK)
                for i in range(2):
                    h = 2 * g + i
                    turned = pltpu.roll(cum_col[...], lax.rem(WIDTH - b * heads - h, WIDTH), 1)
                    c = jnp.broadcast_to(turned[:, :1], (BLOCK, WIDTH))
                    col[h, b] = c
                    end = c[BLOCK - 1 :, :]
                    weighted = (kvb[g, 0, rows, i * WIDTH : (i + 1) * WIDTH].astype(F32) * jnp.exp(end - c)).astype(BF16)
                    v = kvb[g, 1, rows, i * WIDTH : (i + 1) * WIDTH]
                    piece = lax.dot_general(weighted, v, (((0,), (0,)), ((), ())), preferred_element_type=F32)
                    loc[h, b] = runs[i]
                    runs[i] = jnp.exp(end) * runs[i] + piece
            for i in range(2):
                tot[2 * g + i] = runs[i]

        def pair_copy(g):
            return send(tot.at[2 * g + 1 - core], pair_in.at[g], pair_s, pair_r.at[g], "seq", sibling)

        def x_copy(g, d):
            return send(xb.at[g, x], xb.at[g, x], x_s, x_r.at[g], "seq", x_peer(d))

        def y_copy(g, d):
            return send(yb.at[g, y], yb.at[g, y], y_s, y_r.at[g], "seq", y_peer(d))

        def ret_copy(g):
            return send(sret.at[g], sin.at[2 * g + core], ret_s, ret_r.at[g], "seq", sibling)

        def ret_got(g):
            return send(sret.at[g], sin.at[2 * g + 1 - core], ret_s, ret_r.at[g], "seq", sibling)

        dec_pair = send(dec, dsib, dp_s, dp_r, "seq", sibling)

        def dx_copy(d):
            return send(dx.at[x], dx.at[x], dx_s, dx_r, "seq", x_peer(d))

        def dy_copy(d):
            return send(dy.at[y], dy.at[y], dy_s, dy_r, "seq", y_peer(d))

        def between(rows, lo, hi):
            total = jnp.zeros((1, WIDTH), F32)
            for i in range(lo + 1, len(rows)):
                total = total + jnp.where(i < hi, rows[i], 0.0)
            return total

        def own_core(g):
            h = 2 * g + core
            mine, other = tot[h], pair_in[g]
            here, there = dec[pl.ds(h, 1), :], dsib[pl.ds(h, 1), :]
            first = core == 0
            return (
                h,
                jnp.where(first, mine, other),
                jnp.where(first, other, mine),
                jnp.where(first, here, there),
                jnp.where(first, there, here),
            )

        def pair_step(g):
            pair_copy(g).wait_recv()

            @pl.when(g == 0)
            def _():
                dec_pair.wait_recv()
                dx[x] = dec[...] + dsib[...]
                for d in range(1, NX):
                    dx_copy(d).start()

            h, first, second, _, second_decay = own_core(g)
            xb[g, x] = (jnp.exp(second_decay) * first + second).astype(xb.dtype)
            for d in range(1, NX):
                x_copy(g, d).start()

        def x_rows(h):
            return [dx[i, pl.ds(h, 1), :] for i in range(NX)]

        def row_step(g):
            @pl.when(g == 0)
            def _():
                got(dx.at[pl.ds(0, NX - 1)], dx_r)
                dy[y] = dx[0] + dx[1] + dx[2] + dx[3]
                for d in range(1, NY):
                    dy_copy(d).start()

            got(xb.at[g, pl.ds(0, NX - 1)], x_r.at[g])
            h = 2 * g + core
            rows = x_rows(h)
            whole = jnp.zeros((WIDTH, WIDTH), F32)
            before = jnp.zeros((WIDTH, WIDTH), F32)
            for i in range(NX):
                piece = xb[g, i].astype(F32)
                whole = whole + jnp.exp(between(rows, i, NX)) * piece
                before = before + jnp.where(i < x, jnp.exp(between(rows, i, x)), 0.0) * piece
            prow[g] = before
            yb[g, y] = whole.astype(yb.dtype)
            for d in range(1, NY):
                y_copy(g, d).start()

        def return_step(g):
            @pl.when(g == 0)
            def _():
                got(dy.at[pl.ds(0, NY - 1)], dy_r)

            got(yb.at[g, pl.ds(0, NY - 1)], y_r.at[g])
            h, first, _, first_decay, _ = own_core(g)
            rows = [dy[i, pl.ds(h, 1), :] for i in range(NY)]
            above = jnp.zeros((WIDTH, WIDTH), F32)
            for i in range(NY):
                above = above + jnp.where(i < y, jnp.exp(between(rows, i, y)), 0.0) * yb[g, i].astype(F32)
            at_first = jnp.exp(between(x_rows(h), -1, x)) * above + prow[g]
            at_second = jnp.exp(first_decay) * at_first + first
            sin[h] = jnp.where(core == 0, at_first, at_second)
            sret[g] = jnp.where(core == 0, at_second, at_first)
            ret_copy(g).start()

        def z_lanes(g):
            return pl.ds(pl.multiple_of(z * features + g * 2 * WIDTH, 2 * WIDTH), 2 * WIDTH)

        def z_copy(g, part, r0, rows, d):
            p = z_peer(d)
            src = att.at[p, pl.ds(r0, rows), pair_lanes(g)]
            return send(src, recv.at[pl.ds(r0, rows), z_lanes(g)], z_s, z_r.at[part], "head", p)

        def own_copy(g, part, r0, rows):
            src = att.at[z, pl.ds(r0, rows), pair_lanes(g)]
            return pltpu.make_async_copy(src, recv.at[pl.ds(r0, rows), z_lanes(g)], own_sem.at[part])

        def ship(g, part, r0, rows):
            for d in (2, 1, 3):
                z_copy(g, part, r0, rows, d).start()
            own_copy(g, part, r0, rows).start()

        def arrived(part, r0, rows):
            got(att.at[pl.ds(0, z_count - 1), pl.ds(r0, rows)], z_r.at[part])
            got(att.at[0, pl.ds(r0, rows)], own_sem.at[part])

        def attend_first(g):
            ret_got(g).wait_recv()
            got(qb.at[g], q_sem.at[g])
            keep = lax.broadcasted_iota(jnp.int32, (HALF, HALF), 1) <= lax.broadcasted_iota(jnp.int32, (HALF, HALF), 0)
            gone = [jnp.zeros((1, WIDTH), F32)] * 2
            for b in range(blocks):
                rows = slice(b * BLOCK, b * BLOCK + HALF)
                for i in range(2):
                    h = 2 * g + i
                    c = col[h, b, :HALF, :]
                    begin = (jnp.exp(gone[i]) * sin[h] + loc[h, b]).astype(BF16)
                    start[h, b] = begin
                    lanes = slice(i * WIDTH, (i + 1) * WIDTH)
                    q = qb[g, rows, lanes]
                    scores = lax.dot_general(q, kvb[g, 0, rows, lanes], (((1,), (1,)), ((), ())), preferred_element_type=F32)
                    spread = jnp.where(keep, c - cum_row[b, 0, pl.ds(h, 1), :], 0.0)
                    weights = jnp.where(keep, scores * jnp.exp(spread), 0.0).astype(BF16)
                    within = jnp.dot(weights, kvb[g, 1, rows, lanes], preferred_element_type=F32)
                    carried = jnp.dot(q, begin, preferred_element_type=F32) * jnp.exp(c)
                    att[b, :HALF, pl.ds(pl.multiple_of(h * WIDTH, WIDTH), WIDTH)] = (within + carried).astype(BF16)
                    gone[i] = gone[i] + col[h, b, BLOCK - 1 :, :]
            ship(g, 0, 0, HALF)

        def attend_second(g):
            keep = lax.broadcasted_iota(jnp.int32, (HALF, BLOCK), 1) <= HALF + lax.broadcasted_iota(
                jnp.int32, (HALF, BLOCK), 0
            )
            for b in range(blocks):
                rows = slice(b * BLOCK, (b + 1) * BLOCK)
                for i in range(2):
                    h = 2 * g + i
                    c = col[h, b, HALF:, :]
                    lanes = slice(i * WIDTH, (i + 1) * WIDTH)
                    q = qb[g, b * BLOCK + HALF : (b + 1) * BLOCK, lanes]
                    scores = lax.dot_general(q, kvb[g, 0, rows, lanes], (((1,), (1,)), ((), ())), preferred_element_type=F32)
                    wide = jnp.concatenate([c, c], axis=1)
                    key_cum = jnp.concatenate([cum_row[b, j, pl.ds(h, 1), :] for j in range(2)], axis=1)
                    spread = jnp.where(keep, wide - key_cum, 0.0)
                    weights = jnp.where(keep, scores * jnp.exp(spread), 0.0).astype(BF16)
                    within = jnp.dot(weights, kvb[g, 1, rows, lanes], preferred_element_type=F32)
                    carried = jnp.dot(q, start[h, b], preferred_element_type=F32) * jnp.exp(c)
                    att[b, HALF:, pl.ds(pl.multiple_of(h * WIDTH, WIDTH), WIDTH)] = (within + carried).astype(BF16)

            ship(g, 1, *TAIL_PARTS[0])

        chunks = z_count * heads

        def gates():
            @pl.loop(0, BLOCK // 16)
            def _(i):
                rows = pl.ds(pl.multiple_of(i * 16, 16), 16)
                for j in range(chunks):
                    lanes = slice(j * WIDTH, (j + 1) * WIDTH)
                    col[j // blocks, j % blocks, rows, :] = gain_ref[:, lanes] * jax.nn.sigmoid(gv[rows, lanes].astype(F32))

        def norm(r0, count):
            @pl.loop(0, count // 16)
            def _(i):
                rows = pl.ds(pl.multiple_of(r0 + i * 16, 16), 16)
                sums = [jnp.zeros((16, WIDTH), F32)] * 4
                for j in range(chunks):
                    wide = recv[rows, j * WIDTH : (j + 1) * WIDTH].astype(F32)
                    sums[j % 4] = sums[j % 4] + wide * wide
                total = (sums[0] + sums[1]) + (sums[2] + sums[3])
                mean = jnp.sum(total, axis=1, keepdims=True) * (1.0 / (z_count * features))
                scale = jnp.broadcast_to(lax.rsqrt(mean + norm_eps), (16, WIDTH))
                for j in range(chunks):
                    lanes = slice(j * WIDTH, (j + 1) * WIDTH)
                    wide = recv[rows, lanes].astype(F32)
                    recv[rows, lanes] = (wide * scale * col[j // blocks, j % blocks, rows, :]).astype(BF16)

        def out_copy(part, r0, rows):
            return pltpu.make_async_copy(recv.at[pl.ds(r0, rows)], out_ref.at[pl.ds(r0, rows)], out_sem.at[part])

        for g in range(AHEAD):
            states(g)
        pl.semaphore_wait(barrier, 1 + (NX - 1) + (NY - 1) + (z_count - 1))
        dec_pair.start()

        @pl.loop(0, LAG_ATT + groups)
        def _(k):
            @pl.when(k < groups)
            def _():
                pair_copy(k).start()

            @pl.when(k >= LAG_ATT)
            def _():
                attend_first(k - LAG_ATT)

            @pl.when((k >= LAG_RET) & (k < LAG_RET + groups))
            def _():
                return_step(k - LAG_RET)

            @pl.when((k >= LAG_Y) & (k < LAG_Y + groups))
            def _():
                row_step(k - LAG_Y)

            @pl.when((k >= 1) & (k < 1 + groups))
            def _():
                pair_step(k - 1)

            @pl.when(k + AHEAD < groups)
            def _():
                states(k + AHEAD)

        @pl.loop(0, groups)
        def _(g):
            attend_second(g)

        for part in range(1, len(TAIL_PARTS)):
            r0, rows = TAIL_PARTS[part]

            @pl.loop(0, groups)
            def _(g):
                ship(g, part + 1, r0, rows)

        gain_copy.wait()
        gate_copy.wait()
        gates()
        parts = ((0, HALF),) + TAIL_PARTS
        for part, (r0, rows) in enumerate(parts):
            arrived(part, r0, rows)
            norm(r0, rows)
            out_copy(part, r0, rows).start()

        got(dec, dp_s)
        got(dx.at[pl.ds(0, NX - 1)], dx_s)
        got(dy.at[pl.ds(0, NY - 1)], dy_s)
        got(pair_in, pair_s)
        got(xb.at[:, pl.ds(0, NX - 1)], x_s)
        got(yb.at[:, pl.ds(0, NY - 1)], y_s)
        got(sret, ret_s)
        got(att.at[pl.ds(0, z_count - 1)], z_s)
        for part, (r0, rows) in enumerate(parts):
            out_copy(part, r0, rows).wait()

    return kernel


def solution(mesh):
    z_count = mesh.shape["head"]

    def on_device(queries, key_rows, value_rows, log_decay, gate_logits, norm_gain):
        local, features = queries.shape
        heads = log_decay.shape[0]
        blocks = local // BLOCK
        groups = heads // 2
        rows, wide = gate_logits.shape
        parts = 1 + len(TAIL_PARTS)
        vmem, dma = pltpu.VMEM, pltpu.SemaphoreType.DMA
        state = (WIDTH, WIDTH)
        return pl.pallas_call(
            make_kernel(heads, blocks, z_count),
            out_shape=jax.ShapeDtypeStruct((rows, wide), BF16),
            in_specs=[pl.BlockSpec(memory_space=pltpu.HBM)] * 6,
            out_specs=pl.BlockSpec(memory_space=pl.ANY),
            scratch_shapes=[
                vmem((groups, local, 2 * WIDTH), BF16),
                vmem((groups, 2, local, 2 * WIDTH), BF16),
                vmem((rows, wide), BF16),
                vmem((heads, local), F32),
                vmem((1, wide), F32),
                vmem((z_count, rows, features), BF16),
                vmem((rows, wide), BF16),
                vmem((blocks, 2, heads, HALF), F32),
                vmem((BLOCK, WIDTH), F32),
                vmem((heads, blocks, BLOCK, WIDTH), F32),
                vmem((heads, blocks) + state, F32),
                vmem((heads, blocks) + state, BF16),
                vmem((heads,) + state, F32),
                vmem((groups,) + state, F32),
                vmem((groups, NX) + state, BF16),
                vmem((groups, NY) + state, BF16),
                vmem((groups,) + state, F32),
                vmem((groups,) + state, F32),
                vmem((heads,) + state, F32),
                vmem((heads, WIDTH), F32),
                vmem((heads, WIDTH), F32),
                vmem((NX, heads, WIDTH), F32),
                vmem((NY, heads, WIDTH), F32),
                dma((groups,)),
                dma((groups,)),
                dma,
                dma,
                dma,
                dma((parts,)),
                dma((parts,)),
                dma,
                dma((groups,)),
                dma,
                dma((groups,)),
                dma,
                dma((groups,)),
                dma,
                dma((groups,)),
                dma,
                dma((parts,)),
                dma,
                dma,
                dma,
                dma,
                dma,
                dma,
            ],
            compiler_params=pltpu.CompilerParams(
                collective_id=0, has_side_effects=True, vmem_limit_bytes=46 * 2**20
            ),
        )(queries, key_rows, value_rows, log_decay, gate_logits, norm_gain[None, :])

    placed = (
        P("seq", "head"),
        P("seq", "head"),
        P("seq", "head"),
        P("head", "seq"),
        P(("seq", "head"), None),
        P(),
    )
    return jax.shard_map(
        on_device, mesh=mesh, in_specs=placed, out_specs=P(("seq", "head"), None), check_vma=False
    )
```

```python
import jax
import jax.numpy as jnp
from jax import lax
from jax.experimental import pallas as pl
from jax.experimental.pallas import tpu as pltpu
from jax.sharding import PartitionSpec as P

BLOCK = 256
HALF = 128
WIDTH = 128
norm_eps = 1e-06

MESH = pl.DeviceIdType.MESH
F32 = jnp.float32
BF16 = jnp.bfloat16

NX = 4
NY = 4
AHEAD = 1
LAG_Y = 4
LAG_RET = 7
LAG_ATT = 8
TAIL_PARTS = ((128, 64), (192, 48), (240, 16))


def make_kernel(heads, blocks, z_count):
    groups = heads // 2
    features = heads * WIDTH

    def kernel(
        q_hbm, k_hbm, v_hbm, ld_hbm, gate_hbm, gain_hbm, out_ref,
        qb, kvb, gv, ld_ref, gain_ref, att, recv, cum_row, cum_col, col, loc, start, tot, pair_in, xb, yb, prow, sret, sin,
        dec, dsib, dx, dy, lead_first, lead_second, w_row, w_before, w_above, lead_row,
        kv_sem, q_sem, ld_sem, gain_sem, gate_sem, out_sem, own_sem,
        pair_s, pair_r, x_s, x_r, y_s, y_r, ret_s, ret_r, z_s, z_r,
        dp_s, dp_r, dx_s, dx_r, dy_s, dy_r,
    ):
        seq = lax.axis_index("seq")
        z = lax.axis_index("head")
        core = lax.rem(seq, 2)
        x = lax.rem(seq // 2, NX)
        y = seq // (2 * NX)
        sibling = seq + 1 - 2 * core

        def x_peer(d):
            return (y * NX + lax.rem(x + d, NX)) * 2 + core

        def y_peer(d):
            return (lax.rem(y + d, NY) * NX + x) * 2 + core

        def z_peer(d):
            return lax.rem(z + d, z_count)

        def send(src, dst, s, r, axis, dev):
            return pltpu.make_async_remote_copy(
                src_ref=src, dst_ref=dst, send_sem=s, recv_sem=r, device_id={axis: dev}, device_id_type=MESH
            )

        def got(ref, sem):
            pltpu.make_async_copy(ref, ref, sem).wait()

        def pair_lanes(g):
            return pl.ds(pl.multiple_of(g * 2 * WIDTH, 2 * WIDTH), 2 * WIDTH)

        barrier = pltpu.get_barrier_semaphore()
        pl.semaphore_signal(barrier, inc=1, device_id={"seq": sibling}, device_id_type=MESH)
        for d in range(1, NX):
            pl.semaphore_signal(barrier, inc=1, device_id={"seq": x_peer(d)}, device_id_type=MESH)
        for d in range(1, NY):
            pl.semaphore_signal(barrier, inc=1, device_id={"seq": y_peer(d)}, device_id_type=MESH)
        for d in range(1, z_count):
            pl.semaphore_signal(barrier, inc=1, device_id={"head": z_peer(d)}, device_id_type=MESH)

        ld_copy = pltpu.make_async_copy(ld_hbm, ld_ref, ld_sem)
        ld_copy.start()

        @pl.loop(0, groups)
        def _(g):
            pltpu.make_async_copy(k_hbm.at[:, pair_lanes(g)], kvb.at[g, 0], kv_sem.at[g]).start()
            pltpu.make_async_copy(v_hbm.at[:, pair_lanes(g)], kvb.at[g, 1], kv_sem.at[g]).start()

        @pl.loop(0, groups)
        def _(g):
            pltpu.make_async_copy(q_hbm.at[:, pair_lanes(g)], qb.at[g], q_sem.at[g]).start()

        gain_copy = pltpu.make_async_copy(gain_hbm, gain_ref, gain_sem)
        gain_copy.start()
        gate_copy = pltpu.make_async_copy(gate_hbm, gv, gate_sem)
        gate_copy.start()

        t_at = lax.broadcasted_iota(jnp.int32, (BLOCK, BLOCK), 0)
        s_at = lax.broadcasted_iota(jnp.int32, (BLOCK, BLOCK), 1)
        lower = (s_at <= t_at).astype(BF16)
        upper = (t_at <= s_at).astype(BF16)

        def thirds(wide):
            pieces = []
            for _ in range(3):
                pieces.append(wide.astype(BF16))
                wide = wide - pieces[-1].astype(F32)
            return pieces

        def add_up(pieces, one):
            return one(pieces[2]) + one(pieces[1]) + one(pieces[0])

        ld_copy.wait()
        ld = thirds(jnp.concatenate([ld_ref[:, b * BLOCK : (b + 1) * BLOCK] for b in range(blocks)], axis=0))
        blank = jnp.zeros((WIDTH - blocks * heads, BLOCK), BF16)
        cum_col[...] = add_up(
            ld,
            lambda p: lax.dot_general(
                lower, jnp.concatenate([p, blank], axis=0), (((1,), (1,)), ((), ())), preferred_element_type=F32
            ),
        )
        ends = add_up(ld, lambda p: jnp.dot(p, jnp.ones((BLOCK, WIDTH), BF16), preferred_element_type=F32))
        total = ends[:heads]
        for b in range(1, blocks):
            total = total + ends[b * heads : (b + 1) * heads]
        dec[...] = total

        def cum_rows():
            running = add_up(ld, lambda p: jnp.dot(p, upper, preferred_element_type=F32))
            for b in range(blocks):
                cum_row[b, 0] = running[b * heads : (b + 1) * heads, :HALF]
                cum_row[b, 1] = running[b * heads : (b + 1) * heads, HALF:]

        def states(g):
            got(kvb.at[g], kv_sem.at[g])
            runs = [jnp.zeros((WIDTH, WIDTH), F32)] * 2
            for b in range(blocks):
                rows = slice(b * BLOCK, (b + 1) * BLOCK)
                for i in range(2):
                    h = 2 * g + i
                    turned = pltpu.roll(cum_col[...], lax.rem(WIDTH - b * heads - h, WIDTH), 1)
                    c = jnp.broadcast_to(turned[:, :1], (BLOCK, WIDTH))
                    col[h, b] = c
                    end = c[BLOCK - 1 :, :]
                    weighted = (kvb[g, 0, rows, i * WIDTH : (i + 1) * WIDTH].astype(F32) * jnp.exp(end - c)).astype(BF16)
                    v = kvb[g, 1, rows, i * WIDTH : (i + 1) * WIDTH]
                    piece = lax.dot_general(weighted, v, (((0,), (0,)), ((), ())), preferred_element_type=F32)
                    loc[h, b] = runs[i]
                    runs[i] = jnp.exp(end) * runs[i] + piece
            for i in range(2):
                tot[2 * g + i] = runs[i]

        def pair_copy(g):
            return send(tot.at[2 * g + 1 - core], pair_in.at[g], pair_s, pair_r.at[g], "seq", sibling)

        def x_copy(g, d):
            return send(xb.at[g, x], xb.at[g, x], x_s, x_r.at[g], "seq", x_peer(d))

        def y_copy(g, d):
            return send(yb.at[g, y], yb.at[g, y], y_s, y_r.at[g], "seq", y_peer(d))

        def ret_copy(g):
            return send(sret.at[g], sin.at[2 * g + core], ret_s, ret_r.at[g], "seq", sibling)

        def ret_got(g):
            return send(sret.at[g], sin.at[2 * g + 1 - core], ret_s, ret_r.at[g], "seq", sibling)

        dec_pair = send(dec, dsib, dp_s, dp_r, "seq", sibling)

        def dx_copy(d):
            return send(dx.at[x], dx.at[x], dx_s, dx_r, "seq", x_peer(d))

        def dy_copy(d):
            return send(dy.at[y], dy.at[y], dy_s, dy_r, "seq", y_peer(d))

        def between(rows, lo, hi):
            total = jnp.zeros((heads, WIDTH), F32)
            for i in range(lo + 1, len(rows)):
                total = total + jnp.where(i < hi, rows[i], 0.0)
            return total

        def own_core(g):
            h = 2 * g + core
            mine, other = tot[h], pair_in[g]
            first = core == 0
            return h, jnp.where(first, mine, other), jnp.where(first, other, mine)

        def pair_decays():
            got(dsib, dp_r)
            here, there = dec[...], dsib[...]
            dx[x] = here + there
            for d in range(1, NX):
                dx_copy(d).start()
            lead_first[...] = jnp.exp(jnp.where(core == 0, here, there))
            lead_second[...] = jnp.exp(jnp.where(core == 0, there, here))

        def row_decays():
            got(dx.at[pl.ds(0, NX - 1)], dx_r)
            rows = [dx[i] for i in range(NX)]
            dy[y] = rows[0] + rows[1] + rows[2] + rows[3]
            for d in range(1, NY):
                dy_copy(d).start()
            for i in range(NX):
                w_row[i] = jnp.exp(between(rows, i, NX))
                w_before[i] = jnp.where(i < x, jnp.exp(between(rows, i, x)), 0.0)
            lead_row[...] = jnp.exp(between(rows, -1, x))

        def all_decays():
            got(dy.at[pl.ds(0, NY - 1)], dy_r)
            rows = [dy[i] for i in range(NY)]
            for i in range(NY):
                w_above[i] = jnp.where(i < y, jnp.exp(between(rows, i, y)), 0.0)

        def pair_step(g):
            @pl.when(g == 0)
            def _():
                pair_decays()

            pair_copy(g).wait_recv()
            h, first, second = own_core(g)
            xb[g, x] = (lead_second[pl.ds(h, 1), :] * first + second).astype(xb.dtype)
            for d in range(1, NX):
                x_copy(g, d).start()

        def row_step(g):
            got(xb.at[g, pl.ds(0, NX - 1)], x_r.at[g])
            h = 2 * g + core

            def mix(weights):
                total = weights[0, pl.ds(h, 1), :] * xb[g, 0].astype(F32)
                for i in range(1, NX):
                    total = total + weights[i, pl.ds(h, 1), :] * xb[g, i].astype(F32)
                return total

            yb[g, y] = mix(w_row).astype(yb.dtype)
            for d in range(1, NY):
                y_copy(g, d).start()
            prow[g] = mix(w_before)

        def return_step(g):
            got(yb.at[g, pl.ds(0, NY - 1)], y_r.at[g])
            h, first, _ = own_core(g)
            above = w_above[0, pl.ds(h, 1), :] * yb[g, 0].astype(F32)
            for i in range(1, NY):
                above = above + w_above[i, pl.ds(h, 1), :] * yb[g, i].astype(F32)
            at_first = lead_row[pl.ds(h, 1), :] * above + prow[g]
            at_second = lead_first[pl.ds(h, 1), :] * at_first + first
            sret[g] = jnp.where(core == 0, at_second, at_first)
            ret_copy(g).start()
            sin[h] = jnp.where(core == 0, at_first, at_second)

        def z_copy(lanes, part, r0, rows, d):
            at, count = lanes
            p = z_peer(d)
            src = att.at[p, pl.ds(r0, rows), pl.ds(pl.multiple_of(at, count), count)]
            dst = recv.at[pl.ds(r0, rows), pl.ds(pl.multiple_of(z * features + at, count), count)]
            return send(src, dst, z_s, z_r.at[part], "head", p)

        def own_copy(lanes, part, r0, rows):
            at, count = lanes
            src = att.at[z, pl.ds(r0, rows), pl.ds(pl.multiple_of(at, count), count)]
            dst = recv.at[pl.ds(r0, rows), pl.ds(pl.multiple_of(z * features + at, count), count)]
            return pltpu.make_async_copy(src, dst, own_sem.at[part])

        def ship(g, part, r0, rows):
            lanes = (g * 2 * WIDTH, 2 * WIDTH)
            for d in (2, 1, 3):
                z_copy(lanes, part, r0, rows, d).start()
            own_copy(lanes, part, r0, rows).start()

        def arrived(part, r0, rows):
            got(att.at[pl.ds(0, z_count - 1), pl.ds(r0, rows)], z_r.at[part])
            got(att.at[0, pl.ds(r0, rows)], own_sem.at[part])

        def attend_first(g):
            got(qb.at[g], q_sem.at[g])
            keep = lax.broadcasted_iota(jnp.int32, (HALF, HALF), 1) <= lax.broadcasted_iota(jnp.int32, (HALF, HALF), 0)
            for i in (core, 1 - core):
                if i is not core:
                    ret_got(g).wait_recv()
                h = 2 * g + i
                gone = jnp.zeros((1, WIDTH), F32)
                lanes = pl.ds(pl.multiple_of(i * WIDTH, WIDTH), WIDTH)
                for b in range(blocks):
                    begin = (jnp.exp(gone) * sin[h] + loc[h, b]).astype(BF16)
                    start[h, b] = begin
                    gone = gone + col[h, b, BLOCK - 1 :, :]
                    rows = slice(b * BLOCK, b * BLOCK + HALF)
                    c = col[h, b, :HALF, :]
                    q = qb[g, rows, lanes]
                    scores = lax.dot_general(q, kvb[g, 0, rows, lanes], (((1,), (1,)), ((), ())), preferred_element_type=F32)
                    spread = jnp.where(keep, c - cum_row[b, 0, pl.ds(h, 1), :], 0.0)
                    weights = jnp.where(keep, scores * jnp.exp(spread), 0.0).astype(BF16)
                    within = jnp.dot(weights, kvb[g, 1, rows, lanes], preferred_element_type=F32)
                    carried = jnp.dot(q, begin, preferred_element_type=F32) * jnp.exp(c)
                    att[b, :HALF, pl.ds(pl.multiple_of(h * WIDTH, WIDTH), WIDTH)] = (within + carried).astype(BF16)
                head_lanes = (h * WIDTH, WIDTH)
                for d in (2, 1, 3):
                    z_copy(head_lanes, 0, 0, HALF, d).start()
                own_copy(head_lanes, 0, 0, HALF).start()

        def attend_second(g):
            keep = lax.broadcasted_iota(jnp.int32, (HALF, BLOCK), 1) <= HALF + lax.broadcasted_iota(
                jnp.int32, (HALF, BLOCK), 0
            )
            for b in range(blocks):
                rows = slice(b * BLOCK, (b + 1) * BLOCK)
                for i in range(2):
                    h = 2 * g + i
                    c = col[h, b, HALF:, :]
                    lanes = slice(i * WIDTH, (i + 1) * WIDTH)
                    q = qb[g, b * BLOCK + HALF : (b + 1) * BLOCK, lanes]
                    scores = lax.dot_general(q, kvb[g, 0, rows, lanes], (((1,), (1,)), ((), ())), preferred_element_type=F32)
                    wide = jnp.concatenate([c, c], axis=1)
                    key_cum = jnp.concatenate([cum_row[b, j, pl.ds(h, 1), :] for j in range(2)], axis=1)
                    spread = jnp.where(keep, wide - key_cum, 0.0)
                    weights = jnp.where(keep, scores * jnp.exp(spread), 0.0).astype(BF16)
                    within = jnp.dot(weights, kvb[g, 1, rows, lanes], preferred_element_type=F32)
                    carried = jnp.dot(q, start[h, b], preferred_element_type=F32) * jnp.exp(c)
                    att[b, HALF:, pl.ds(pl.multiple_of(h * WIDTH, WIDTH), WIDTH)] = (within + carried).astype(BF16)

            ship(g, 1, *TAIL_PARTS[0])

        chunks = z_count * heads

        def gates():
            @pl.loop(0, BLOCK // 16)
            def _(i):
                rows = pl.ds(pl.multiple_of(i * 16, 16), 16)
                for j in range(chunks):
                    lanes = slice(j * WIDTH, (j + 1) * WIDTH)
                    col[j // blocks, j % blocks, rows, :] = gain_ref[:, lanes] * jax.nn.sigmoid(gv[rows, lanes].astype(F32))

        def norm(r0, count):
            @pl.loop(0, count // 16)
            def _(i):
                rows = pl.ds(pl.multiple_of(r0 + i * 16, 16), 16)
                sums = [jnp.zeros((16, WIDTH), F32)] * 4
                for j in range(chunks):
                    wide = recv[rows, j * WIDTH : (j + 1) * WIDTH].astype(F32)
                    sums[j % 4] = sums[j % 4] + wide * wide
                total = (sums[0] + sums[1]) + (sums[2] + sums[3])
                mean = jnp.sum(total, axis=1, keepdims=True) * (1.0 / (z_count * features))
                scale = jnp.broadcast_to(lax.rsqrt(mean + norm_eps), (16, WIDTH))
                for j in range(chunks):
                    lanes = slice(j * WIDTH, (j + 1) * WIDTH)
                    wide = recv[rows, lanes].astype(F32)
                    recv[rows, lanes] = (wide * scale * col[j // blocks, j % blocks, rows, :]).astype(BF16)

        def out_copy(part, r0, rows):
            return pltpu.make_async_copy(recv.at[pl.ds(r0, rows)], out_ref.at[pl.ds(r0, rows)], out_sem.at[part])

        for g in range(AHEAD):
            states(g)
        pl.semaphore_wait(barrier, 1 + (NX - 1) + (NY - 1) + (z_count - 1))
        dec_pair.start()

        @pl.loop(0, LAG_ATT + groups)
        def _(k):
            @pl.when(k < groups)
            def _():
                pair_copy(k).start()

            @pl.when(k >= LAG_ATT)
            def _():
                attend_first(k - LAG_ATT)

            @pl.when((k >= LAG_RET) & (k < LAG_RET + groups))
            def _():
                return_step(k - LAG_RET)

            @pl.when((k >= LAG_Y) & (k < LAG_Y + groups))
            def _():
                row_step(k - LAG_Y)

            @pl.when((k >= 1) & (k < 1 + groups))
            def _():
                pair_step(k - 1)

            @pl.when(k + AHEAD < groups)
            def _():
                states(k + AHEAD)

            @pl.when(k == 1)
            def _():
                cum_rows()

            @pl.when(k == LAG_Y - 1)
            def _():
                row_decays()

            @pl.when(k == LAG_RET - 1)
            def _():
                all_decays()

        @pl.loop(0, groups)
        def _(g):
            attend_second(g)

        for part in range(1, len(TAIL_PARTS)):
            r0, rows = TAIL_PARTS[part]

            @pl.loop(0, groups)
            def _(g):
                ship(g, part + 1, r0, rows)

        gain_copy.wait()
        gate_copy.wait()
        gates()
        parts = ((0, HALF),) + TAIL_PARTS
        for part, (r0, rows) in enumerate(parts):
            arrived(part, r0, rows)
            norm(r0, rows)
            out_copy(part, r0, rows).start()

        got(dec, dp_s)
        got(dx.at[pl.ds(0, NX - 1)], dx_s)
        got(dy.at[pl.ds(0, NY - 1)], dy_s)
        got(pair_in, pair_s)
        got(xb.at[:, pl.ds(0, NX - 1)], x_s)
        got(yb.at[:, pl.ds(0, NY - 1)], y_s)
        got(sret, ret_s)
        got(att.at[pl.ds(0, z_count - 1)], z_s)
        for part, (r0, rows) in enumerate(parts):
            out_copy(part, r0, rows).wait()

    return kernel


def solution(mesh):
    z_count = mesh.shape["head"]

    def on_device(queries, key_rows, value_rows, log_decay, gate_logits, norm_gain):
        local, features = queries.shape
        heads = log_decay.shape[0]
        blocks = local // BLOCK
        groups = heads // 2
        rows, wide = gate_logits.shape
        parts = 1 + len(TAIL_PARTS)
        vmem, dma = pltpu.VMEM, pltpu.SemaphoreType.DMA
        state = (WIDTH, WIDTH)
        given = (queries, key_rows, value_rows, log_decay, gate_logits, norm_gain[None, :])
        return pl.pallas_call(
            make_kernel(heads, blocks, z_count),
            out_shape=jax.ShapeDtypeStruct((rows, wide), BF16),
            in_specs=[pl.BlockSpec(memory_space=pltpu.HBM)] * 6,
            out_specs=pl.BlockSpec(memory_space=pl.ANY),
            scratch_shapes=[
                vmem((groups, local, 2 * WIDTH), BF16),
                vmem((groups, 2, local, 2 * WIDTH), BF16),
                vmem((rows, wide), BF16),
                vmem((heads, local), F32),
                vmem((1, wide), F32),
                vmem((z_count, rows, features), BF16),
                vmem((rows, wide), BF16),
                vmem((blocks, 2, heads, HALF), F32),
                vmem((BLOCK, WIDTH), F32),
                vmem((heads, blocks, BLOCK, WIDTH), F32),
                vmem((heads, blocks) + state, F32),
                vmem((heads, blocks) + state, BF16),
                vmem((heads,) + state, F32),
                vmem((groups,) + state, F32),
                vmem((groups, NX) + state, BF16),
                vmem((groups, NY) + state, BF16),
                vmem((groups,) + state, F32),
                vmem((groups,) + state, F32),
                vmem((heads,) + state, F32),
                vmem((heads, WIDTH), F32),
                vmem((heads, WIDTH), F32),
                vmem((NX, heads, WIDTH), F32),
                vmem((NY, heads, WIDTH), F32),
                vmem((heads, WIDTH), F32),
                vmem((heads, WIDTH), F32),
                vmem((NX, heads, WIDTH), F32),
                vmem((NX, heads, WIDTH), F32),
                vmem((NY, heads, WIDTH), F32),
                vmem((heads, WIDTH), F32),
                dma((groups,)),
                dma((groups,)),
                dma,
                dma,
                dma,
                dma((parts,)),
                dma((parts,)),
                dma,
                dma((groups,)),
                dma,
                dma((groups,)),
                dma,
                dma((groups,)),
                dma,
                dma((groups,)),
                dma,
                dma((parts,)),
                dma,
                dma,
                dma,
                dma,
                dma,
                dma,
            ],
            compiler_params=pltpu.CompilerParams(
                collective_id=0, has_side_effects=True, vmem_limit_bytes=46 * 2**20
            ),
        )(*[pltpu.with_memory_space_constraint(a, pltpu.HBM) for a in given])

    placed = (
        P("seq", "head"),
        P("seq", "head"),
        P("seq", "head"),
        P("head", "seq"),
        P(("seq", "head"), None),
        P(),
    )
    return jax.shard_map(
        on_device, mesh=mesh, in_specs=placed, out_specs=P(("seq", "head"), None), check_vma=False
    )
```

```python
import jax
import jax.numpy as jnp
from jax import lax
from jax.experimental import pallas as pl
from jax.experimental.pallas import tpu as pltpu
from jax.sharding import PartitionSpec as P

BLOCK = 256
HALF = 128
WIDTH = 128
norm_eps = 1e-06

MESH = pl.DeviceIdType.MESH
F32 = jnp.float32
BF16 = jnp.bfloat16

NX = 4
NY = 4
AHEAD = 1
LAG_Y = 4
LAG_RET = 7
LAG_ATT = 8
EARLY = 1
TAIL_PARTS = ((128, 64), (192, 48), (240, 16))


def make_kernel(heads, blocks, z_count):
    groups = heads // 2
    features = heads * WIDTH

    def kernel(
        q_hbm, k_hbm, v_hbm, ld_hbm, gate_hbm, gain_hbm, out_ref,
        qb, kvb, gv, ld_ref, gain_ref, att, recv, cum_row, cum_col, col, loc, start, tot, pair_in, xb, yb, prow, sret, sin,
        dec, dsib, dx, dy, lead_first, lead_second, w_row, w_before, w_above, lead_row, q_out, q_in, state_out, state_in,
        kv_sem, q_sem, ld_sem, gain_sem, gate_sem, out_sem, own_sem,
        pair_s, pair_r, x_s, x_r, y_s, y_r, ret_s, ret_r, z_s, z_r,
        dp_s, dp_r, dx_s, dx_r, dy_s, dy_r, qz_s, qz_r, qz_own, sz_s, sz_r,
    ):
        seq = lax.axis_index("seq")
        z = lax.axis_index("head")
        core = lax.rem(seq, 2)
        x = lax.rem(seq // 2, NX)
        y = seq // (2 * NX)
        sibling = seq + 1 - 2 * core

        def x_peer(d):
            return (y * NX + lax.rem(x + d, NX)) * 2 + core

        def y_peer(d):
            return (lax.rem(y + d, NY) * NX + x) * 2 + core

        def z_peer(d):
            return lax.rem(z + d, z_count)

        def send(src, dst, s, r, axis, dev):
            return pltpu.make_async_remote_copy(
                src_ref=src, dst_ref=dst, send_sem=s, recv_sem=r, device_id={axis: dev}, device_id_type=MESH
            )

        def got(ref, sem):
            pltpu.make_async_copy(ref, ref, sem).wait()

        def pair_lanes(g):
            return pl.ds(pl.multiple_of(g * 2 * WIDTH, 2 * WIDTH), 2 * WIDTH)

        barrier = pltpu.get_barrier_semaphore()
        pl.semaphore_signal(barrier, inc=1, device_id={"seq": sibling}, device_id_type=MESH)
        for d in range(1, NX):
            pl.semaphore_signal(barrier, inc=1, device_id={"seq": x_peer(d)}, device_id_type=MESH)
        for d in range(1, NY):
            pl.semaphore_signal(barrier, inc=1, device_id={"seq": y_peer(d)}, device_id_type=MESH)
        for d in range(1, z_count):
            pl.semaphore_signal(barrier, inc=1, device_id={"head": z_peer(d)}, device_id_type=MESH)

        ld_copy = pltpu.make_async_copy(ld_hbm, ld_ref, ld_sem)
        ld_copy.start()

        @pl.loop(0, groups)
        def _(g):
            pltpu.make_async_copy(k_hbm.at[:, pair_lanes(g)], kvb.at[g, 0], kv_sem.at[g]).start()
            pltpu.make_async_copy(v_hbm.at[:, pair_lanes(g)], kvb.at[g, 1], kv_sem.at[g]).start()

        @pl.loop(0, groups)
        def _(g):
            pltpu.make_async_copy(q_hbm.at[:, pair_lanes(g)], qb.at[g], q_sem.at[g]).start()

        gain_copy = pltpu.make_async_copy(gain_hbm, gain_ref, gain_sem)
        gain_copy.start()
        gate_copy = pltpu.make_async_copy(gate_hbm, gv, gate_sem)
        gate_copy.start()

        t_at = lax.broadcasted_iota(jnp.int32, (BLOCK, BLOCK), 0)
        s_at = lax.broadcasted_iota(jnp.int32, (BLOCK, BLOCK), 1)
        lower = (s_at <= t_at).astype(BF16)
        upper = (t_at <= s_at).astype(BF16)

        def thirds(wide):
            pieces = []
            for _ in range(3):
                pieces.append(wide.astype(BF16))
                wide = wide - pieces[-1].astype(F32)
            return pieces

        def add_up(pieces, one):
            return one(pieces[2]) + one(pieces[1]) + one(pieces[0])

        ld_copy.wait()
        ld = thirds(jnp.concatenate([ld_ref[:, b * BLOCK : (b + 1) * BLOCK] for b in range(blocks)], axis=0))
        blank = jnp.zeros((WIDTH - blocks * heads, BLOCK), BF16)
        cum_col[...] = add_up(
            ld,
            lambda p: lax.dot_general(
                lower, jnp.concatenate([p, blank], axis=0), (((1,), (1,)), ((), ())), preferred_element_type=F32
            ),
        )
        ends = add_up(ld, lambda p: jnp.dot(p, jnp.ones((BLOCK, WIDTH), BF16), preferred_element_type=F32))
        total = ends[:heads]
        for b in range(1, blocks):
            total = total + ends[b * heads : (b + 1) * heads]
        dec[...] = total

        def cum_rows():
            running = add_up(ld, lambda p: jnp.dot(p, upper, preferred_element_type=F32))
            for b in range(blocks):
                cum_row[b, 0] = running[b * heads : (b + 1) * heads, :HALF]
                cum_row[b, 1] = running[b * heads : (b + 1) * heads, HALF:]

        def states(g):
            got(kvb.at[g], kv_sem.at[g])
            runs = [jnp.zeros((WIDTH, WIDTH), F32)] * 2
            for b in range(blocks):
                rows = slice(b * BLOCK, (b + 1) * BLOCK)
                for i in range(2):
                    h = 2 * g + i
                    turned = pltpu.roll(cum_col[...], lax.rem(WIDTH - b * heads - h, WIDTH), 1)
                    c = jnp.broadcast_to(turned[:, :1], (BLOCK, WIDTH))
                    col[h, b] = c
                    end = c[BLOCK - 1 :, :]
                    weighted = (kvb[g, 0, rows, i * WIDTH : (i + 1) * WIDTH].astype(F32) * jnp.exp(end - c)).astype(BF16)
                    v = kvb[g, 1, rows, i * WIDTH : (i + 1) * WIDTH]
                    piece = lax.dot_general(weighted, v, (((0,), (0,)), ((), ())), preferred_element_type=F32)
                    loc[h, b] = runs[i]
                    runs[i] = jnp.exp(end) * runs[i] + piece
            for i in range(2):
                tot[2 * g + i] = runs[i]

        def pair_copy(g):
            return send(tot.at[2 * g + 1 - core], pair_in.at[g], pair_s, pair_r.at[g], "seq", sibling)

        def x_copy(g, d):
            return send(xb.at[g, x], xb.at[g, x], x_s, x_r.at[g], "seq", x_peer(d))

        def y_copy(g, d):
            return send(yb.at[g, y], yb.at[g, y], y_s, y_r.at[g], "seq", y_peer(d))

        def ret_copy(g):
            return send(sret.at[g], sin.at[2 * g + core], ret_s, ret_r.at[g], "seq", sibling)

        def ret_got(g):
            return send(sret.at[g], sin.at[2 * g + 1 - core], ret_s, ret_r.at[g], "seq", sibling)

        dec_pair = send(dec, dsib, dp_s, dp_r, "seq", sibling)

        def dx_copy(d):
            return send(dx.at[x], dx.at[x], dx_s, dx_r, "seq", x_peer(d))

        def dy_copy(d):
            return send(dy.at[y], dy.at[y], dy_s, dy_r, "seq", y_peer(d))

        def between(rows, lo, hi):
            total = jnp.zeros((heads, WIDTH), F32)
            for i in range(lo + 1, len(rows)):
                total = total + jnp.where(i < hi, rows[i], 0.0)
            return total

        def own_core(g):
            h = 2 * g + core
            mine, other = tot[h], pair_in[g]
            first = core == 0
            return h, jnp.where(first, mine, other), jnp.where(first, other, mine)

        def pair_decays():
            got(dsib, dp_r)
            here, there = dec[...], dsib[...]
            dx[x] = here + there
            for d in range(1, NX):
                dx_copy(d).start()
            lead_first[...] = jnp.exp(jnp.where(core == 0, here, there))
            lead_second[...] = jnp.exp(jnp.where(core == 0, there, here))

        def row_decays():
            got(dx.at[pl.ds(0, NX - 1)], dx_r)
            rows = [dx[i] for i in range(NX)]
            dy[y] = rows[0] + rows[1] + rows[2] + rows[3]
            for d in range(1, NY):
                dy_copy(d).start()
            for i in range(NX):
                w_row[i] = jnp.exp(between(rows, i, NX))
                w_before[i] = jnp.where(i < x, jnp.exp(between(rows, i, x)), 0.0)
            lead_row[...] = jnp.exp(between(rows, -1, x))

        def all_decays():
            got(dy.at[pl.ds(0, NY - 1)], dy_r)
            rows = [dy[i] for i in range(NY)]
            for i in range(NY):
                w_above[i] = jnp.where(i < y, jnp.exp(between(rows, i, y)), 0.0)

        def pair_step(g):
            @pl.when(g == 0)
            def _():
                pair_decays()

            pair_copy(g).wait_recv()
            h, first, second = own_core(g)
            xb[g, x] = (lead_second[pl.ds(h, 1), :] * first + second).astype(xb.dtype)
            for d in range(1, NX):
                x_copy(g, d).start()

        def row_step(g):
            got(xb.at[g, pl.ds(0, NX - 1)], x_r.at[g])
            h = 2 * g + core

            def mix(weights):
                total = weights[0, pl.ds(h, 1), :] * xb[g, 0].astype(F32)
                for i in range(1, NX):
                    total = total + weights[i, pl.ds(h, 1), :] * xb[g, i].astype(F32)
                return total

            yb[g, y] = mix(w_row).astype(yb.dtype)
            for d in range(1, NY):
                y_copy(g, d).start()
            prow[g] = mix(w_before)

        def return_step(g):
            got(yb.at[g, pl.ds(0, NY - 1)], y_r.at[g])
            h, first, _ = own_core(g)
            above = w_above[0, pl.ds(h, 1), :] * yb[g, 0].astype(F32)
            for i in range(1, NY):
                above = above + w_above[i, pl.ds(h, 1), :] * yb[g, i].astype(F32)
            at_first = lead_row[pl.ds(h, 1), :] * above + prow[g]
            at_second = lead_first[pl.ds(h, 1), :] * at_first + first
            sret[g] = jnp.where(core == 0, at_second, at_first)
            ret_copy(g).start()
            sin[h] = jnp.where(core == 0, at_first, at_second)

        def z_copy(lanes, part, r0, rows, d):
            at, count = lanes
            p = z_peer(d)
            src = att.at[p, pl.ds(r0, rows), pl.ds(pl.multiple_of(at, count), count)]
            dst = recv.at[pl.ds(r0, rows), pl.ds(pl.multiple_of(z * features + at, count), count)]
            return send(src, dst, z_s, z_r.at[part], "head", p)

        def own_copy(lanes, part, r0, rows):
            at, count = lanes
            src = att.at[z, pl.ds(r0, rows), pl.ds(pl.multiple_of(at, count), count)]
            dst = recv.at[pl.ds(r0, rows), pl.ds(pl.multiple_of(z * features + at, count), count)]
            return pltpu.make_async_copy(src, dst, own_sem.at[part])

        def ship(g, part, r0, rows):
            lanes = (g * 2 * WIDTH, 2 * WIDTH)
            for d in (2, 1, 3):
                z_copy(lanes, part, r0, rows, d).start()
            own_copy(lanes, part, r0, rows).start()

        rest = pl.ds(0, (groups - 1) * 2 * WIDTH)
        early_part = 1 + len(TAIL_PARTS)
        early_lanes = (EARLY * 2 * WIDTH, 2 * WIDTH)

        def early_query(d):
            return send(q_out.at[z_peer(d)], q_in.at[z], qz_s, qz_r, "head", z_peer(d))

        def early_own():
            return pltpu.make_async_copy(q_out.at[z], q_in.at[z], qz_own)

        def late_state(d):
            return send(state_out, state_in.at[z], sz_s, sz_r, "head", z_peer(d))

        def early_attend():
            got(qb.at[EARLY], q_sem.at[EARLY])
            for i in range(2):
                h = 2 * EARLY + i
                lanes = slice(i * WIDTH, (i + 1) * WIDTH)
                gone = jnp.zeros((1, WIDTH), F32)
                for b in range(blocks):
                    begin = loc[h, b].astype(BF16)
                    for half in range(2):
                        count = (half + 1) * HALF
                        keys = slice(b * BLOCK, b * BLOCK + count)
                        mine = slice(half * HALF, count)
                        c = col[h, b, mine, :]
                        q = qb[EARLY, b * BLOCK + half * HALF : b * BLOCK + count, lanes]
                        scores = lax.dot_general(
                            q, kvb[EARLY, 0, keys, lanes], (((1,), (1,)), ((), ())), preferred_element_type=F32
                        )
                        keep = lax.broadcasted_iota(jnp.int32, (HALF, count), 1) <= half * HALF + (
                            lax.broadcasted_iota(jnp.int32, (HALF, count), 0)
                        )
                        wide = jnp.concatenate([c] * (half + 1), axis=1)
                        key_cum = jnp.concatenate([cum_row[b, j, h : h + 1, :] for j in range(half + 1)], axis=1)
                        spread = jnp.where(keep, wide - key_cum, 0.0)
                        weights = jnp.where(keep, scores * jnp.exp(spread), 0.0).astype(BF16)
                        within = jnp.dot(weights, kvb[EARLY, 1, keys, lanes], preferred_element_type=F32)
                        carried = jnp.dot(q, begin, preferred_element_type=F32) * jnp.exp(c)
                        att[b, mine, h * WIDTH : (h + 1) * WIDTH] = (within + carried).astype(BF16)
                        q_out[b, mine, lanes] = (q.astype(F32) * jnp.exp(c + gone)).astype(BF16)
                    gone = gone + col[h, b, BLOCK - 1 :, :]
            for d in (2, 1, 3):
                z_copy(early_lanes, early_part, 0, BLOCK, d).start()
                early_query(d).start()
            own_copy(early_lanes, early_part, 0, BLOCK).start()
            early_own().start()

        def late_states():
            ret_got(EARLY).wait_recv()
            for i in range(2):
                state_out[i] = sin[2 * EARLY + i].astype(BF16)
            state_in[z] = state_out[...]
            for d in (2, 1, 3):
                late_state(d).start()

        def finish_early():
            first = pl.ds(0, 2 * WIDTH)
            got(att.at[pl.ds(0, z_count - 1), :, first], z_r.at[early_part])
            got(att.at[0, :, first], own_sem.at[early_part])
            got(q_in.at[pl.ds(0, z_count - 1)], qz_r)
            early_own().wait()
            got(state_in.at[pl.ds(0, z_count - 1)], sz_r)
            for source in range(z_count):
                for i in range(2):
                    at = source * features + (2 * EARLY + i) * WIDTH
                    lanes = slice(at, at + WIDTH)
                    more = jnp.dot(
                        q_in[source, :, i * WIDTH : (i + 1) * WIDTH], state_in[source, i], preferred_element_type=F32
                    )
                    recv[:, lanes] = (recv[:, lanes].astype(F32) + more).astype(BF16)

        def arrived(part, r0, rows):
            got(att.at[pl.ds(0, z_count - 1), pl.ds(r0, rows), rest], z_r.at[part])
            got(att.at[0, pl.ds(r0, rows), rest], own_sem.at[part])

        def attend_first(g):
            got(qb.at[g], q_sem.at[g])
            keep = lax.broadcasted_iota(jnp.int32, (HALF, HALF), 1) <= lax.broadcasted_iota(jnp.int32, (HALF, HALF), 0)
            for i in (core, 1 - core):
                if i is not core:
                    ret_got(g).wait_recv()
                h = 2 * g + i
                gone = jnp.zeros((1, WIDTH), F32)
                lanes = pl.ds(pl.multiple_of(i * WIDTH, WIDTH), WIDTH)
                for b in range(blocks):
                    begin = (jnp.exp(gone) * sin[h] + loc[h, b]).astype(BF16)
                    start[h, b] = begin
                    gone = gone + col[h, b, BLOCK - 1 :, :]
                    rows = slice(b * BLOCK, b * BLOCK + HALF)
                    c = col[h, b, :HALF, :]
                    q = qb[g, rows, lanes]
                    scores = lax.dot_general(q, kvb[g, 0, rows, lanes], (((1,), (1,)), ((), ())), preferred_element_type=F32)
                    spread = jnp.where(keep, c - cum_row[b, 0, pl.ds(h, 1), :], 0.0)
                    weights = jnp.where(keep, scores * jnp.exp(spread), 0.0).astype(BF16)
                    within = jnp.dot(weights, kvb[g, 1, rows, lanes], preferred_element_type=F32)
                    carried = jnp.dot(q, begin, preferred_element_type=F32) * jnp.exp(c)
                    att[b, :HALF, pl.ds(pl.multiple_of(h * WIDTH, WIDTH), WIDTH)] = (within + carried).astype(BF16)
                head_lanes = (h * WIDTH, WIDTH)
                for d in (2, 1, 3):
                    z_copy(head_lanes, 0, 0, HALF, d).start()
                own_copy(head_lanes, 0, 0, HALF).start()

        def attend_second(g):
            keep = lax.broadcasted_iota(jnp.int32, (HALF, BLOCK), 1) <= HALF + lax.broadcasted_iota(
                jnp.int32, (HALF, BLOCK), 0
            )
            for b in range(blocks):
                rows = slice(b * BLOCK, (b + 1) * BLOCK)
                for i in range(2):
                    h = 2 * g + i
                    c = col[h, b, HALF:, :]
                    lanes = slice(i * WIDTH, (i + 1) * WIDTH)
                    q = qb[g, b * BLOCK + HALF : (b + 1) * BLOCK, lanes]
                    scores = lax.dot_general(q, kvb[g, 0, rows, lanes], (((1,), (1,)), ((), ())), preferred_element_type=F32)
                    wide = jnp.concatenate([c, c], axis=1)
                    key_cum = jnp.concatenate([cum_row[b, j, pl.ds(h, 1), :] for j in range(2)], axis=1)
                    spread = jnp.where(keep, wide - key_cum, 0.0)
                    weights = jnp.where(keep, scores * jnp.exp(spread), 0.0).astype(BF16)
                    within = jnp.dot(weights, kvb[g, 1, rows, lanes], preferred_element_type=F32)
                    carried = jnp.dot(q, start[h, b], preferred_element_type=F32) * jnp.exp(c)
                    att[b, HALF:, pl.ds(pl.multiple_of(h * WIDTH, WIDTH), WIDTH)] = (within + carried).astype(BF16)

            ship(g, 1, *TAIL_PARTS[0])

        chunks = z_count * heads

        def gates():
            @pl.loop(0, BLOCK // 16)
            def _(i):
                rows = pl.ds(pl.multiple_of(i * 16, 16), 16)
                for j in range(chunks):
                    lanes = slice(j * WIDTH, (j + 1) * WIDTH)
                    col[j // blocks, j % blocks, rows, :] = gain_ref[:, lanes] * jax.nn.sigmoid(gv[rows, lanes].astype(F32))

        def norm(r0, count):
            @pl.loop(0, count // 16)
            def _(i):
                rows = pl.ds(pl.multiple_of(r0 + i * 16, 16), 16)
                sums = [jnp.zeros((16, WIDTH), F32)] * 4
                for j in range(chunks):
                    wide = recv[rows, j * WIDTH : (j + 1) * WIDTH].astype(F32)
                    sums[j % 4] = sums[j % 4] + wide * wide
                total = (sums[0] + sums[1]) + (sums[2] + sums[3])
                mean = jnp.sum(total, axis=1, keepdims=True) * (1.0 / (z_count * features))
                scale = jnp.broadcast_to(lax.rsqrt(mean + norm_eps), (16, WIDTH))
                for j in range(chunks):
                    lanes = slice(j * WIDTH, (j + 1) * WIDTH)
                    wide = recv[rows, lanes].astype(F32)
                    recv[rows, lanes] = (wide * scale * col[j // blocks, j % blocks, rows, :]).astype(BF16)

        def out_copy(part, r0, rows):
            return pltpu.make_async_copy(recv.at[pl.ds(r0, rows)], out_ref.at[pl.ds(r0, rows)], out_sem.at[part])

        for g in range(AHEAD):
            states(g)
        cum_rows()
        pl.semaphore_wait(barrier, 1 + (NX - 1) + (NY - 1) + (z_count - 1))
        dec_pair.start()

        @pl.loop(0, LAG_ATT + groups)
        def _(k):
            @pl.when(k < groups)
            def _():
                pair_copy(k).start()

            @pl.when(k == LAG_ATT + EARLY)
            def _():
                late_states()

            @pl.when((k >= LAG_ATT) & (k != LAG_ATT + EARLY))
            def _():
                attend_first(k - LAG_ATT)

            @pl.when((k >= LAG_RET) & (k < LAG_RET + groups))
            def _():
                return_step(k - LAG_RET)

            @pl.when((k >= LAG_Y) & (k < LAG_Y + groups))
            def _():
                row_step(k - LAG_Y)

            @pl.when((k >= 1) & (k < 1 + groups))
            def _():
                pair_step(k - 1)

            @pl.when(k == 1)
            def _():
                early_attend()

            @pl.when(k + AHEAD < groups)
            def _():
                states(k + AHEAD)

            @pl.when(k == LAG_Y - 1)
            def _():
                row_decays()

            @pl.when(k == LAG_RET - 1)
            def _():
                all_decays()

        @pl.loop(0, groups)
        def _(g):
            @pl.when(g != EARLY)
            def _():
                attend_second(g)

        for part in range(1, len(TAIL_PARTS)):
            r0, rows = TAIL_PARTS[part]

            @pl.loop(0, groups)
            def _(g):
                @pl.when(g != EARLY)
                def _():
                    ship(g, part + 1, r0, rows)

        gain_copy.wait()
        gate_copy.wait()
        gates()
        finish_early()
        parts = ((0, HALF),) + TAIL_PARTS
        for part, (r0, rows) in enumerate(parts):
            arrived(part, r0, rows)
            norm(r0, rows)
            out_copy(part, r0, rows).start()

        got(dec, dp_s)
        got(dx.at[pl.ds(0, NX - 1)], dx_s)
        got(dy.at[pl.ds(0, NY - 1)], dy_s)
        got(pair_in, pair_s)
        got(xb.at[:, pl.ds(0, NX - 1)], x_s)
        got(yb.at[:, pl.ds(0, NY - 1)], y_s)
        got(sret, ret_s)
        got(att.at[pl.ds(0, z_count - 1)], z_s)
        got(q_out.at[pl.ds(0, z_count - 1)], qz_s)
        got(state_in.at[pl.ds(0, z_count - 1)], sz_s)
        for part, (r0, rows) in enumerate(parts):
            out_copy(part, r0, rows).wait()

    return kernel


def solution(mesh):
    z_count = mesh.shape["head"]

    def on_device(queries, key_rows, value_rows, log_decay, gate_logits, norm_gain):
        local, features = queries.shape
        heads = log_decay.shape[0]
        blocks = local // BLOCK
        groups = heads // 2
        rows, wide = gate_logits.shape
        parts = 1 + len(TAIL_PARTS)
        vmem, dma = pltpu.VMEM, pltpu.SemaphoreType.DMA
        state = (WIDTH, WIDTH)
        given = (queries, key_rows, value_rows, log_decay, gate_logits, norm_gain[None, :])
        return pl.pallas_call(
            make_kernel(heads, blocks, z_count),
            out_shape=jax.ShapeDtypeStruct((rows, wide), BF16),
            in_specs=[pl.BlockSpec(memory_space=pltpu.HBM)] * 6,
            out_specs=pl.BlockSpec(memory_space=pl.ANY),
            scratch_shapes=[
                vmem((groups, local, 2 * WIDTH), BF16),
                vmem((groups, 2, local, 2 * WIDTH), BF16),
                vmem((rows, wide), BF16),
                vmem((heads, local), F32),
                vmem((1, wide), F32),
                vmem((z_count, rows, features), BF16),
                vmem((rows, wide), BF16),
                vmem((blocks, 2, heads, HALF), F32),
                vmem((BLOCK, WIDTH), F32),
                vmem((heads, blocks, BLOCK, WIDTH), F32),
                vmem((heads, blocks) + state, F32),
                vmem((heads, blocks) + state, BF16),
                vmem((heads,) + state, F32),
                vmem((groups,) + state, F32),
                vmem((groups, NX) + state, BF16),
                vmem((groups, NY) + state, BF16),
                vmem((groups,) + state, F32),
                vmem((groups,) + state, F32),
                vmem((heads,) + state, F32),
                vmem((heads, WIDTH), F32),
                vmem((heads, WIDTH), F32),
                vmem((NX, heads, WIDTH), F32),
                vmem((NY, heads, WIDTH), F32),
                vmem((heads, WIDTH), F32),
                vmem((heads, WIDTH), F32),
                vmem((NX, heads, WIDTH), F32),
                vmem((NX, heads, WIDTH), F32),
                vmem((NY, heads, WIDTH), F32),
                vmem((heads, WIDTH), F32),
                vmem((z_count, rows, 2 * WIDTH), BF16),
                vmem((z_count, rows, 2 * WIDTH), BF16),
                vmem((2,) + state, BF16),
                vmem((z_count, 2) + state, BF16),
                dma((groups,)),
                dma((groups,)),
                dma,
                dma,
                dma,
                dma((parts,)),
                dma((parts + 1,)),
                dma,
                dma((groups,)),
                dma,
                dma((groups,)),
                dma,
                dma((groups,)),
                dma,
                dma((groups,)),
                dma,
                dma((parts + 1,)),
                dma,
                dma,
                dma,
                dma,
                dma,
                dma,
                dma,
                dma,
                dma,
                dma,
                dma,
            ],
            compiler_params=pltpu.CompilerParams(
                collective_id=0, has_side_effects=True, vmem_limit_bytes=48 * 2**20
            ),
        )(*[pltpu.with_memory_space_constraint(a, pltpu.HBM) for a in given])

    placed = (
        P("seq", "head"),
        P("seq", "head"),
        P("seq", "head"),
        P("head", "seq"),
        P(("seq", "head"), None),
        P(),
    )
    return jax.shard_map(
        on_device, mesh=mesh, in_specs=placed, out_specs=P(("seq", "head"), None), check_vma=False
    )
```
